32 devices in a mesh: tile: 8 (over z, y), cuts: 4 (over x, core).
Axes of the slice: x: 2, y: 2, z: 4, core: 2. Of those that a mesh axis runs over, the one named last changes fastest.
Arguments:
- object_slices: float32 [8, 2, 2048, 256], P('cuts', None, 'tile'), may hold values from -1 to 1, as said below
- probe_field: float32 [2, 256, 256], replicated, may hold values from -6 to 6
- row_offsets: int32 [32], P('tile'), may hold values from 0 to 255, as said below
- columns: int32 [32], P('tile'), may hold values from 0 to 0
- counts: int32 [8], P('tile'), may hold values from 1 to 4, 16 in all
- amplitudes: bfloat16 [32, 256, 256], P('tile'), may hold values from 0.25 to 4
Outputs:
- new_object: float32 [8, 2, 2048, 256], P('cuts', None, 'tile')
The draws below stay inside these ranges and needn't reach their ends.
Inputs may be any that keep to these rules, and one draw needn't show every extreme that they name: `row_offsets`: the patch of slot k of block b starts at object row b * 256 + value; in the last block values are at most 0, so every patch lies inside the object and inside its own tile and the next one. `counts`: block b uses its first value slots; the others are padding. The values sum to 16. `object_slices`: every entry has magnitude at most 1.
All inputs are finite; a program needn't handle non-finite values.
Results may differ from the reference program's by a relative error of at most 0.015.
Values may be sent and summed in bfloat16 or wider, within the bound.
A program may use at most 64 MiB of HBM per device.

```python
import math
import jax
import jax.numpy as jnp
import numpy as np
from jax import lax

PAT = 256
TR = 256
OW = 256
CAP = 4
ITERS = 2
TILES = 8
SLICES = 8


def draw_object_slices(key, part):
    first_key, second_key = jax.random.split(jax.random.fold_in(key, 11))
    shape = (SLICES, TILES * TR, OW)
    magnitude = jax.random.uniform(first_key, shape, jnp.float32, 0.75, 1.0)
    phase = jax.random.uniform(second_key, shape, jnp.float32, -math.pi, math.pi)
    return jnp.stack([magnitude * jnp.cos(phase), magnitude * jnp.sin(phase)], axis=1)


def draw_row_offsets(key, part):
    block = jnp.arange(TILES * CAP, dtype=jnp.int32) // CAP
    upper = jnp.where(block == TILES - 1, TR - PAT + 1, TR).astype(jnp.int32)
    values = jax.random.randint(jax.random.fold_in(key, 23), (TILES * CAP,), 0, upper, dtype=jnp.int32)
    values = values.at[0].set(0)
    return values.at[1].set(TR - 1)


def draw_columns(key, part):
    values = jax.random.randint(jax.random.fold_in(key, 37), (TILES * CAP,), 0, OW - PAT + 1, dtype=jnp.int32)
    values = values.at[0].set(0)
    return values.at[1].set(OW - PAT)


def level_of(own_key, dims, cuts, least, top_value):
    def one(dim, shards_of):
        draws = jax.random.uniform(jax.random.fold_in(jax.random.fold_in(own_key, 6), dim), (shards_of,), jnp.float32, least / len(cuts), top_value / len(cuts))
        return jnp.repeat(jnp.exp(draws), dims[dim] // shards_of).reshape((-1,) + (1,) * (len(dims) - dim - 1))

    level = one(*cuts[0])
    for cut in cuts[1:]:
        level = level * one(*cut)
    return level


def length_profile(count, total, bound, skew):
    weights = [(1 << 20) // math.isqrt(rank ** skew) + 1 for rank in range(2, count + 1)]
    surplus, given = total - bound - (count - 1), [1] * (count - 1)
    while surplus > 0:
        free = [i for i in range(count - 1) if given[i] < bound]
        mass, remaining = sum([weights[i] for i in free]), surplus
        for i in free:
            extra = min(bound - given[i], max(1, remaining * weights[i] // mass), surplus)
            given[i] = given[i] + extra
            surplus = surplus - extra
    return np.array([bound] + given)


def ragged_sizes(rng, number_of, total, limit, lean):
    if number_of == 2:
        one = jax.random.randint(rng, (), max(1, total - limit), min(limit, total - 1) + 1)
        return jnp.stack([one, total - one])
    tallies = jnp.asarray(length_profile(number_of, total, limit, lean), jnp.int32)
    twos = (number_of - 1) // 2
    donor, receiver = tallies[1:1 + 2 * twos:2], tallies[2:2 + 2 * twos:2]
    slack = jnp.minimum(donor - 1, limit - receiver)
    passed = jax.random.randint(jax.random.fold_in(rng, 1), (twos,), 0, 1 << 20) % (slack + 1)
    tallies = tallies.at[1:1 + 2 * twos:2].set(donor - passed).at[2:2 + 2 * twos:2].set(receiver + passed)
    return tallies[jax.random.permutation(jax.random.fold_in(rng, 2), number_of)]


def bell_draw(rng, extent, spread, most, kind=jnp.bfloat16):
    entries = jax.random.normal(rng, extent, jnp.float32) * spread
    return jnp.minimum(jnp.maximum(entries, -most), most).astype(kind)


def setup_inputs(seed: int = 0) -> dict:
    key_of = jax.random.split(jax.random.key(seed), 7)
    object_slices = draw_object_slices(jax.random.fold_in(key_of[6], 71), 0)
    probe_field = bell_draw(key_of[1], (2, PAT, PAT), 1.0, 6.0, jnp.float32)
    row_offsets = draw_row_offsets(jax.random.fold_in(key_of[6], 71), 0)
    columns = draw_columns(jax.random.fold_in(key_of[6], 71), 0)
    counts = ragged_sizes(key_of[4], TILES, TILES * CAP // 2, CAP, 2).astype(jnp.int32)
    amplitudes = jnp.clip(jnp.exp(math.log(4.0) - 2.7725887 * jax.random.uniform(key_of[5], (TILES * CAP, PAT, PAT), jnp.float32) ** level_of(key_of[5], (TILES * CAP, PAT, PAT), ((0, 8),), -0.2, 0.2)), 0.25, 4.0).astype(jnp.bfloat16)
    return {"object_slices": object_slices, "probe_field": probe_field, "row_offsets": row_offsets, "columns": columns, "counts": counts, "amplitudes": amplitudes}


object_rate = 0.25

def tables(size):
    index = jnp.arange(size, dtype=jnp.int32)
    angle = (index[:, None] * index[None, :] % size).astype(jnp.float32) * (2.0 * math.pi / size)
    cosine = jnp.cos(angle)
    sine = jnp.sin(angle)
    signed = jnp.where(index < size // 2, index, index - size)
    phase = (signed * signed % (8 * size)).astype(jnp.float32) * (-math.pi / (4.0 * size))
    filter_re = jnp.cos(phase)
    filter_im = jnp.sin(phase)
    highest = lax.Precision.HIGHEST
    kernel_re = (jnp.dot(filter_re, cosine, precision=highest) - jnp.dot(filter_im, sine, precision=highest)) / size
    kernel_im = (jnp.dot(filter_re, sine, precision=highest) + jnp.dot(filter_im, cosine, precision=highest)) / size
    offset = (index[:, None] - index[None, :]) % size
    norm_factor = 1.0 / math.sqrt(size)
    return ((cosine * norm_factor).astype(jnp.bfloat16), (-sine * norm_factor).astype(jnp.bfloat16), kernel_re[offset].astype(jnp.bfloat16), kernel_im[offset].astype(jnp.bfloat16))

def through(real_table, imag_table, field_re, field_im):
    highest = lax.Precision.HIGHEST
    table_re = real_table.astype(jnp.float32)
    table_im = imag_table.astype(jnp.float32)
    field_re = field_re.astype(jnp.float32)
    field_im = field_im.astype(jnp.float32)
    left = lambda table, field: jnp.einsum('ab,nbc->nac', table, field, precision=highest)
    right = lambda field, table: jnp.einsum('nab,bc->nac', field, table, precision=highest)
    inner_re = left(table_re, field_re) - left(table_im, field_im)
    inner_im = left(table_re, field_im) + left(table_im, field_re)
    inner_re = lax.optimization_barrier(inner_re.astype(jnp.bfloat16)).astype(jnp.float32)
    inner_im = lax.optimization_barrier(inner_im.astype(jnp.bfloat16)).astype(jnp.float32)
    outer_re = right(inner_re, table_re) - right(inner_im, table_im)
    outer_im = right(inner_re, table_im) + right(inner_im, table_re)
    return (outer_re, outer_im)

def propagate(real_table, imag_table, stacked):
    out_re, out_im = through(real_table, imag_table, stacked[:, 0], stacked[:, 1])
    return jnp.stack([out_re, out_im], axis=1).astype(jnp.bfloat16)

def block_pass(current, probe, offsets, cols, count, amps, block, tabs):
    four_re, four_im, kernel_re, kernel_im = tabs
    zero = jnp.zeros((), jnp.int32)
    rows = (block * TR + offsets).astype(jnp.int32)
    windows = jax.vmap(lambda row_start, column: lax.dynamic_slice(current, (zero, zero, row_start.astype(jnp.int32), column.astype(jnp.int32)), (SLICES, 2, PAT, PAT)))(rows, cols)
    mask = (jnp.arange(CAP, dtype=jnp.int32) < count).astype(jnp.float32)
    field = jnp.broadcast_to(probe.astype(jnp.bfloat16)[None], (CAP, 2, PAT, PAT))
    saved = []
    product = field
    for layer_index in range(SLICES):
        saved.append(field)
        window = windows[:, layer_index]
        field32 = field.astype(jnp.float32)
        real = field32[:, 0] * window[:, 0] - field32[:, 1] * window[:, 1]
        imag = field32[:, 0] * window[:, 1] + field32[:, 1] * window[:, 0]
        product = jnp.stack([real, imag], axis=1).astype(jnp.bfloat16)
        if layer_index < SLICES - 1:
            field = propagate(kernel_re, kernel_im, product)
    far_re, far_im = through(four_re, four_im, product[:, 0], product[:, 1])
    modulus = jnp.sqrt(far_re * far_re + far_im * far_im + 1.0)
    factor = mask[:, None, None] * (1.0 - amps.astype(jnp.float32) / modulus)
    chi = jnp.stack([far_re * factor, far_im * factor], axis=1).astype(jnp.bfloat16)
    gradient = propagate(four_re, -four_im, chi)
    terms = [None] * SLICES
    for layer_index in reversed(range(SLICES)):
        field32 = saved[layer_index].astype(jnp.float32)
        grad32 = gradient.astype(jnp.float32)
        window = windows[:, layer_index]
        terms[layer_index] = jnp.stack([field32[:, 0] * grad32[:, 0] + field32[:, 1] * grad32[:, 1], field32[:, 0] * grad32[:, 1] - field32[:, 1] * grad32[:, 0]], axis=1)
        if layer_index > 0:
            adjoint = jnp.stack([window[:, 0] * grad32[:, 0] + window[:, 1] * grad32[:, 1], window[:, 0] * grad32[:, 1] - window[:, 1] * grad32[:, 0]], axis=1)
            gradient = propagate(kernel_re, -kernel_im, adjoint.astype(jnp.bfloat16))
    patch_grads = jnp.stack(terms, axis=1)
    return (patch_grads, rows)

def reference(object_slices, probe_field, row_offsets, columns, counts, amplitudes):
    tabs = tables(PAT)
    offsets = row_offsets.reshape(TILES, CAP).astype(jnp.int32)
    cols = columns.reshape(TILES, CAP).astype(jnp.int32)
    amps = amplitudes.reshape(TILES, CAP, PAT, PAT)
    current = object_slices
    probe = probe_field
    zero = jnp.zeros((), jnp.int32)
    for iteration in range(ITERS):

        def scan_tile(grads, inputs, current=current):
            block, block_offsets, block_cols, count, block_amps = inputs
            patch_grads, rows = block_pass(current, probe, block_offsets, block_cols, count, block_amps, block, tabs)

            def add_patch(slot, grads):
                corner = (zero, zero, rows[slot].astype(jnp.int32), block_cols[slot].astype(jnp.int32))
                region = lax.dynamic_slice(grads, corner, (SLICES, 2, PAT, PAT)) + patch_grads[slot]
                return lax.dynamic_update_slice(grads, region, corner)
            grads = lax.fori_loop(0, CAP, add_patch, grads)
            return (grads, None)
        start = jnp.zeros(current.shape, current.dtype)
        grads, unused = lax.scan(scan_tile, start, (jnp.arange(TILES, dtype=jnp.int32), offsets, cols, counts.astype(jnp.int32), amps))
        current = current - object_rate * grads
    return current
```

```python
import functools
import math

import jax
import jax.numpy as jnp
import numpy as np
from jax import lax
from jax.experimental import pallas as pl
from jax.experimental.pallas import tpu as pltpu
from jax.sharding import PartitionSpec as P

PAT = 256
ITERS = 2
RATE = 0.25
BF16 = jnp.bfloat16
F32 = jnp.float32
MESH = pl.DeviceIdType.MESH


def tables(size):
    index = np.arange(size)
    angle = (index[:, None] * index[None, :] % size) * (2.0 * math.pi / size)
    cosine, sine = np.cos(angle), np.sin(angle)
    signed = np.where(index < size // 2, index, index - size)
    phase = (signed * signed % (8 * size)) * (-math.pi / (4.0 * size))
    filter_re, filter_im = np.cos(phase), np.sin(phase)
    kernel_re = (filter_re @ cosine - filter_im @ sine) / size
    kernel_im = (filter_re @ sine + filter_im @ cosine) / size
    offset = (index[:, None] - index[None, :]) % size
    norm = 1.0 / math.sqrt(size)

    def rounded(a):
        return a.astype(np.float32).astype(jnp.bfloat16)

    def pair(re, im):
        re, im = rounded(re), rounded(im)
        left = np.concatenate([np.concatenate([re, -im], 1), np.concatenate([im, re], 1)], 0)
        right = np.concatenate([np.concatenate([re, im], 1), np.concatenate([-im, re], 1)], 0)
        return np.stack([left, right])

    return pair(kernel_re[offset], kernel_im[offset]), pair(cosine * norm, -sine * norm)


def transform(left, right, stacked):
    mid = jnp.dot(left, stacked, preferred_element_type=F32).astype(BF16)
    mid = jnp.concatenate([mid[:PAT], mid[PAT:]], axis=1)
    full = jnp.dot(mid, right, preferred_element_type=F32)
    return full[:, :PAT], full[:, PAT:]


def rows_of(re, im):
    return jnp.concatenate([re.astype(BF16), im.astype(BF16)], axis=0)


def shifted(block, shift):
    turned = pltpu.roll(block, (8 - shift) & 7, 1)
    within = lax.broadcasted_iota(jnp.int32, turned[1:].shape, 1) < 8 - shift
    return jnp.where(within, turned[:-1], turned[1:])


def kernel(
    places, counts, obj, probe, amps, prop, four, out,
    ext, grads, padded, win, psi, sent_psi, got_g, sent_g, sent_dn, sent_up, got_dn, got_up,
    psi_ss, psi_rs, g_ss, g_rs, dn_ss, dn_rs, up_ss, up_rs,
):
    depth, _, rows, width = obj.shape
    slots = amps.shape[0]
    own, reach, pat = rows // 8, (rows + PAT) // 8, PAT // 8
    cut, cuts = lax.axis_index("cuts"), lax.axis_size("cuts")
    tile, tiles = lax.axis_index("tile"), lax.axis_size("tile")
    not_first, not_last = cut > 0, cut < cuts - 1
    has_before, has_after = tile > 0, tile < tiles - 1

    barrier = pltpu.get_barrier_semaphore()
    for there, where in (
        (not_first, {"cuts": cut - 1}),
        (not_last, {"cuts": cut + 1}),
        (has_before, {"tile": tile - 1}),
        (has_after, {"tile": tile + 1}),
    ):
        @pl.when(there)
        def _(where=where):
            pl.semaphore_signal(barrier, inc=1, device_id=where, device_id_type=MESH)
    neighbours = sum(
        there.astype(jnp.int32) for there in (not_first, not_last, has_before, has_after)
    )
    pl.semaphore_wait(barrier, neighbours)

    def copy_psi(it, slot):
        return pltpu.make_async_remote_copy(
            sent_psi.at[it, slot], psi.at[slot, 0], psi_ss.at[it, slot], psi_rs.at[it, slot],
            device_id={"cuts": cut + 1}, device_id_type=MESH)

    def copy_g(it, slot):
        return pltpu.make_async_remote_copy(
            sent_g.at[it, slot], got_g.at[it, slot], g_ss.at[it, slot], g_rs.at[it, slot],
            device_id={"cuts": cut - 1}, device_id_type=MESH)

    def copy_dn(stage, l):
        return pltpu.make_async_remote_copy(
            sent_dn.at[stage, l], got_dn.at[stage, l], dn_ss.at[stage, l], dn_rs.at[stage, l],
            device_id={"tile": tile - 1}, device_id_type=MESH)

    def copy_up(it, l):
        return pltpu.make_async_remote_copy(
            sent_up.at[it, l], got_up.at[it, l], up_ss.at[it, l], up_rs.at[it, l],
            device_id={"tile": tile + 1}, device_id_type=MESH)

    for l in range(depth):
        sent_dn[0, l] = obj[l, :, :PAT].astype(BF16)

        @pl.when(has_before)
        def _(l=l):
            copy_dn(0, l).start()

    for stage in range(ITERS):
        @pl.when(jnp.logical_not(has_after))
        def _(stage=stage):
            got_dn[stage] = jnp.zeros(got_dn.shape[1:], BF16)

        @pl.when(jnp.logical_not(has_before))
        def _(stage=stage):
            got_up[stage] = jnp.zeros(got_up.shape[1:], BF16)

    @pl.when(jnp.logical_not(not_first))
    def _():
        start = rows_of(probe[0], probe[1])
        for slot in range(slots):
            psi[slot, 0] = start

    for part in range(2):
        padded[part, :pat] = jnp.zeros((pat, 8, width), F32)
        padded[part, 2 * pat :] = jnp.zeros((own + 1, 8, width), F32)

    def eights(block):
        return block.reshape(block.shape[:-2] + (block.shape[-2] // 8, 8, width))

    def flat(block):
        return block.reshape(block.shape[:-3] + (block.shape[-3] * 8, width))

    def prepare(it, l):
        @pl.when(has_after)
        def _():
            copy_dn(it, l).wait_recv()

        @pl.when(it == 0)
        def _():
            ext[l, :, :own] = eights(obj[l])
            ext[l, :, own:] = eights(got_dn[0, l].astype(F32))

        @pl.when(it > 0)
        def _():
            @pl.when(has_before)
            def _():
                copy_up(it - 1, l).wait_recv()

            ext[l, :, :own] = updated(it - 1, l)
            ext[l, :, own:] -= RATE * (grads[l, :, own:] + eights(got_dn[it, l].astype(F32)))

        grads[l] = jnp.zeros(grads.shape[1:], F32)

    def updated(it, l):
        top = ext[l, :, :pat] - RATE * (grads[l, :, :pat] + eights(got_up[it, l].astype(F32)))
        if own == pat:
            return top
        rest = ext[l, :, pat:own] - RATE * grads[l, :, pat:own]
        return jnp.concatenate([top, rest], axis=1)

    def forward(it, slot):
        @pl.when(not_first)
        def _():
            copy_psi(it, slot).wait_recv()

        for l in range(depth):
            @pl.when(slot == 0)
            def _(l=l):
                prepare(it, l)

            place = places[0, slot]
            for part in range(2):
                block = ext[l, part, pl.ds(place, pat + 1)]
                win[slot, l, part] = flat(shifted(block, places[1, slot]))
            w_re, w_im = win[slot, l, 0], win[slot, l, 1]
            f_re = psi[slot, l, :PAT].astype(F32)
            f_im = psi[slot, l, PAT:].astype(F32)
            u = rows_of(f_re * w_re - f_im * w_im, f_re * w_im + f_im * w_re)
            if l < depth - 1:
                psi[slot, l + 1] = rows_of(*transform(prop[0], prop[1], u))
                continue

            @pl.when(not_last)
            def _():
                sent_psi[it, slot] = rows_of(*transform(prop[0], prop[1], u))
                copy_psi(it, slot).start()

            @pl.when(jnp.logical_not(not_last))
            def _():
                far_re, far_im = transform(four[0], four[1], u)
                mask = jnp.where(slot < counts[0], 1.0, 0.0).astype(F32)
                modulus = jnp.sqrt(far_re * far_re + far_im * far_im + 1.0)
                factor = mask * (1.0 - amps[slot].astype(F32) / modulus)
                chi = rows_of(far_re * factor, far_im * factor)
                got_g[it, slot] = rows_of(*transform(four[1], four[0], chi))

    def backward(it, slot):
        @pl.when(not_last)
        def _():
            copy_g(it, slot).wait_recv()

        g = got_g[it, slot]
        for l in reversed(range(depth)):
            g_re, g_im = g[:PAT].astype(F32), g[PAT:].astype(F32)
            w_re, w_im = win[slot, l, 0], win[slot, l, 1]
            d = rows_of(w_re * g_re + w_im * g_im, w_re * g_im - w_im * g_re)
            if l > 0:
                g = rows_of(*transform(prop[1], prop[0], d))
            f_re = psi[slot, l, :PAT].astype(F32)
            f_im = psi[slot, l, PAT:].astype(F32)
            if l == 0:
                @pl.when(not_first)
                def _():
                    sent_g[it, slot] = rows_of(*transform(prop[1], prop[0], d))
                    copy_g(it, slot).start()

            padded[0, pat : 2 * pat] = eights(f_re * g_re + f_im * g_im)
            padded[1, pat : 2 * pat] = eights(f_re * g_im - f_im * g_re)
            place = places[2, slot]
            for part in range(2):
                block = padded[part, pl.ds(place, reach + 1)]
                grads[l, part] += shifted(block, places[3, slot])

            @pl.when(slot == slots - 1)
            def _(l=l):
                @pl.when(has_after)
                def _():
                    sent_up[it, l] = flat(grads[l, :, own:]).astype(BF16)
                    copy_up(it, l).start()

                @pl.when(jnp.logical_and(has_before, it < ITERS - 1))
                def _():
                    sent_dn[it + 1, l] = flat(grads[l, :, :pat]).astype(BF16)
                    copy_dn(it + 1, l).start()

    lag = jnp.minimum(cuts - 1 - cut, 2)
    lag = jnp.where(lag == 2, slots - 1, lag)

    def step(index, _):
        it, at = index // (2 * slots - 1), index % (2 * slots - 1)

        @pl.when(at < slots)
        def _():
            forward(it, at)

        @pl.when(jnp.logical_and(at >= lag, at < lag + slots))
        def _():
            backward(it, at - lag)

        return 0

    lax.fori_loop(0, ITERS * (2 * slots - 1), step, 0)

    for l in reversed(range(depth)):
        @pl.when(has_before)
        def _(l=l):
            copy_up(ITERS - 1, l).wait_recv()

        out[l] = flat(updated(ITERS - 1, l))

    for it in range(ITERS):
        for slot in range(slots):
            @pl.when(not_last)
            def _(it=it, slot=slot):
                copy_psi(it, slot).wait_send()

            @pl.when(not_first)
            def _(it=it, slot=slot):
                copy_g(it, slot).wait_send()

        for l in range(depth):
            @pl.when(has_after)
            def _(it=it, l=l):
                copy_up(it, l).wait_send()

            @pl.when(has_before)
            def _(it=it, l=l):
                copy_dn(it, l).wait_send()


def local(object_slices, probe_field, row_offsets, columns, counts, amplitudes):
    depth, _, rows, width = object_slices.shape
    slots = amplitudes.shape[0]
    prop, four = tables(PAT)
    back = PAT - row_offsets
    places = jnp.stack([row_offsets // 8, row_offsets % 8, back // 8, back % 8])
    dma = pltpu.SemaphoreType.DMA
    vmem, smem = pltpu.VMEM, pltpu.SMEM
    return pl.pallas_call(
        kernel,
        out_shape=jax.ShapeDtypeStruct(object_slices.shape, F32),
        in_specs=[pl.BlockSpec(memory_space=smem)] * 2 + [pl.BlockSpec(memory_space=vmem)] * 5,
        out_specs=pl.BlockSpec(memory_space=vmem),
        scratch_shapes=[
            vmem((depth, 2, (rows + PAT) // 8, 8, width), F32),
            vmem((depth, 2, (rows + PAT) // 8, 8, width), F32),
            vmem((2, (2 * PAT + rows) // 8 + 1, 8, width), F32),
            vmem((slots, depth, 2, PAT, width), F32),
            vmem((slots, depth, 2 * PAT, PAT), BF16),
            vmem((ITERS, slots, 2 * PAT, PAT), BF16),
            vmem((ITERS, slots, 2 * PAT, PAT), BF16),
            vmem((ITERS, slots, 2 * PAT, PAT), BF16),
            vmem((ITERS, depth, 2, PAT, width), BF16),
            vmem((ITERS, depth, 2, PAT, width), BF16),
            vmem((ITERS, depth, 2, PAT, width), BF16),
            vmem((ITERS, depth, 2, PAT, width), BF16),
            dma((ITERS, slots)), dma((ITERS, slots)),
            dma((ITERS, slots)), dma((ITERS, slots)),
            dma((ITERS, depth)), dma((ITERS, depth)),
            dma((ITERS, depth)), dma((ITERS, depth)),
        ],
        compiler_params=pltpu.CompilerParams(
            collective_id=0, has_side_effects=True, vmem_limit_bytes=48 * 1024 * 1024),
    )(places, counts, object_slices, probe_field, amplitudes, jnp.asarray(prop), jnp.asarray(four))


def solution(mesh):
    in_specs = (
        P("cuts", None, "tile", None),
        P(),
        P("tile"),
        P("tile"),
        P("tile"),
        P("tile", None, None),
    )
    out_specs = P("cuts", None, "tile", None)
    return jax.shard_map(local, mesh=mesh, in_specs=in_specs, out_specs=out_specs, check_vma=False)
```

```python
import functools
import math

import jax
import jax.numpy as jnp
import numpy as np
from jax import lax
from jax.experimental import pallas as pl
from jax.experimental.pallas import tpu as pltpu
from jax.sharding import PartitionSpec as P

PAT = 256
ITERS = 2
RATE = 0.25
BF16 = jnp.bfloat16
F32 = jnp.float32
MESH = pl.DeviceIdType.MESH


def tables(size):
    index = np.arange(size)
    angle = (index[:, None] * index[None, :] % size) * (2.0 * math.pi / size)
    cosine, sine = np.cos(angle), np.sin(angle)
    signed = np.where(index < size // 2, index, index - size)
    phase = (signed * signed % (8 * size)) * (-math.pi / (4.0 * size))
    filter_re, filter_im = np.cos(phase), np.sin(phase)
    kernel_re = (filter_re @ cosine - filter_im @ sine) / size
    kernel_im = (filter_re @ sine + filter_im @ cosine) / size
    offset = (index[:, None] - index[None, :]) % size
    norm = 1.0 / math.sqrt(size)

    def rounded(a):
        return a.astype(np.float32).astype(jnp.bfloat16)

    def pair(re, im):
        re, im = rounded(re), rounded(im)
        left = np.concatenate([np.concatenate([re, -im], 1), np.concatenate([im, re], 1)], 0)
        right = np.concatenate([np.concatenate([re, im], 1), np.concatenate([-im, re], 1)], 0)
        return np.stack([left, right])

    return pair(kernel_re[offset], kernel_im[offset]), pair(cosine * norm, -sine * norm)


def transform(left, right, stacked):
    mid = jnp.dot(left, stacked, preferred_element_type=F32).astype(BF16)
    mid = jnp.concatenate([mid[:PAT], mid[PAT:]], axis=1)
    full = jnp.dot(mid, right, preferred_element_type=F32)
    return full[:, :PAT], full[:, PAT:]


def rows_of(re, im):
    return jnp.concatenate([re.astype(BF16), im.astype(BF16)], axis=0)


def shifted(block, shift):
    turned = pltpu.roll(block, (8 - shift) & 7, 1)
    within = lax.broadcasted_iota(jnp.int32, turned[1:].shape, 1) < 8 - shift
    return jnp.where(within, turned[:-1], turned[1:])


def kernel(
    places, counts, obj_in, probe_in, amps_in, prop_in, four_in, out,
    obj, probe, amps, prop, four, ext, grads, padded, win, psi, kept_g, sent_psi, got_g, sent_g, sent_dn, sent_up, got_dn, got_up,
    psi_ss, psi_rs, g_ss, g_rs, dn_ss, dn_rs, up_ss, up_rs,
    in_sems, go,
):
    depth, _, rows, width = obj.shape
    slots = amps.shape[0]
    own, reach, pat = rows // 8, (rows + PAT) // 8, PAT // 8
    cut, cuts = lax.axis_index("cuts"), lax.axis_size("cuts")
    tile, tiles = lax.axis_index("tile"), lax.axis_size("tile")
    not_first, not_last = cut > 0, cut < cuts - 1
    has_before, has_after = tile > 0, tile < tiles - 1

    slice_loads = [
        pltpu.make_async_copy(obj_in.at[l], obj.at[l], in_sems.at[l]) for l in range(depth)
    ]
    loads = [
        pltpu.make_async_copy(src, dst, in_sems.at[depth + i])
        for i, (src, dst) in enumerate(
            ((prop_in, prop), (probe_in, probe), (four_in, four), (amps_in, amps)))
    ]
    for load in slice_loads + loads:
        load.start()

    barrier = pltpu.get_barrier_semaphore()
    for there, where in (
        (not_first, {"cuts": cut - 1}),
        (not_last, {"cuts": cut + 1}),
        (has_before, {"tile": tile - 1}),
        (has_after, {"tile": tile + 1}),
    ):
        @pl.when(there)
        def _(where=where):
            pl.semaphore_signal(barrier, inc=1, device_id=where, device_id_type=MESH)
    neighbours = sum(
        there.astype(jnp.int32) for there in (not_first, not_last, has_before, has_after)
    )
    pl.semaphore_wait(barrier, neighbours)

    def copy_psi(it, slot):
        return pltpu.make_async_remote_copy(
            sent_psi.at[it, slot], psi.at[it, slot, 0], psi_ss.at[it, slot], psi_rs.at[it, slot],
            device_id={"cuts": cut + 1}, device_id_type=MESH)

    def copy_g(it, slot):
        return pltpu.make_async_remote_copy(
            sent_g.at[it, slot], got_g.at[it, slot], g_ss.at[it, slot], g_rs.at[it, slot],
            device_id={"cuts": cut - 1}, device_id_type=MESH)

    def copy_dn(stage, l):
        return pltpu.make_async_remote_copy(
            sent_dn.at[stage, l], got_dn.at[stage, l], dn_ss.at[stage, l], dn_rs.at[stage, l],
            device_id={"tile": tile - 1}, device_id_type=MESH)

    def copy_up(it, l):
        return pltpu.make_async_remote_copy(
            sent_up.at[it, l], got_up.at[it, l], up_ss.at[it, l], up_rs.at[it, l],
            device_id={"tile": tile + 1}, device_id_type=MESH)

    for l in range(depth):
        slice_loads[l].wait()
        sent_dn[0, l] = obj[l, :, :PAT].astype(BF16)
        if l == 0:
            @pl.when(cut == 1)
            def _():
                pl.semaphore_wait(go, 1)

        @pl.when(has_before)
        def _(l=l):
            copy_dn(0, l).start()

    for load in loads:
        load.wait()

    for stage in range(ITERS):
        @pl.when(jnp.logical_not(has_after))
        def _(stage=stage):
            got_dn[stage] = jnp.zeros(got_dn.shape[1:], BF16)

        @pl.when(jnp.logical_not(has_before))
        def _(stage=stage):
            got_up[stage] = jnp.zeros(got_up.shape[1:], BF16)

    @pl.when(jnp.logical_not(not_first))
    def _():
        start = rows_of(probe[0], probe[1])
        for it in range(ITERS):
            for slot in range(slots):
                psi[it, slot, 0] = start

        @pl.when(has_before)
        def _():
            for l in range(depth):
                copy_dn(0, l).wait_send()

        if cuts > 1:
            pl.semaphore_signal(go, inc=1, device_id={"cuts": cut + 1}, device_id_type=MESH)

    for part in range(2):
        padded[part, :pat] = jnp.zeros((pat, 8, width), F32)
        padded[part, 2 * pat :] = jnp.zeros((own + 1, 8, width), F32)

    def eights(block):
        return block.reshape(block.shape[:-2] + (block.shape[-2] // 8, 8, width))

    def flat(block):
        return block.reshape(block.shape[:-3] + (block.shape[-3] * 8, width))

    def prepare(it, l):
        @pl.when(has_after)
        def _():
            copy_dn(it, l).wait_recv()

        @pl.when(it == 0)
        def _():
            ext[l, :, :own] = eights(obj[l])
            ext[l, :, own:] = eights(got_dn[0, l].astype(F32))

        @pl.when(it > 0)
        def _():
            @pl.when(has_before)
            def _():
                copy_up(it - 1, l).wait_recv()

            ext[l, :, :own] = updated(it - 1, l)
            ext[l, :, own:] -= RATE * (grads[l, :, own:] + eights(got_dn[it, l].astype(F32)))

    def extract(slot, l):
        place = places[0, slot]
        for part in range(2):
            block = ext[l, part, pl.ds(place, pat + 1)]
            win[slot, l, part] = flat(shifted(block, places[1, slot]))

    def updated(it, l):
        top = ext[l, :, :pat] - RATE * (grads[l, :, :pat] + eights(got_up[it, l].astype(F32)))
        if own == pat:
            return top
        rest = ext[l, :, pat:own] - RATE * grads[l, :, pat:own]
        return jnp.concatenate([top, rest], axis=1)

    def forward(it, slot):
        @pl.when(jnp.logical_and(not_first, slot == 0))
        def _():
            for l in range(depth):
                prepare(it, l)
                for each in range(slots):
                    extract(each, l)

        @pl.when(not_first)
        def _():
            copy_psi(it, slot).wait_recv()

        for l in range(depth):
            @pl.when(jnp.logical_not(not_first))
            def _(l=l):
                @pl.when(slot == 0)
                def _():
                    prepare(it, l)

                extract(slot, l)

            w_re, w_im = win[slot, l, 0], win[slot, l, 1]
            f_re = psi[it, slot, l, :PAT].astype(F32)
            f_im = psi[it, slot, l, PAT:].astype(F32)
            u = rows_of(f_re * w_re - f_im * w_im, f_re * w_im + f_im * w_re)
            if l < depth - 1:
                psi[it, slot, l + 1] = rows_of(*transform(prop[0], prop[1], u))
                continue

            @pl.when(not_last)
            def _():
                sent_psi[it, slot] = rows_of(*transform(prop[0], prop[1], u))
                copy_psi(it, slot).start()

            @pl.when(jnp.logical_not(not_last))
            def _():
                far_re, far_im = transform(four[0], four[1], u)
                mask = jnp.where(slot < counts[0], 1.0, 0.0).astype(F32)
                modulus = jnp.sqrt(far_re * far_re + far_im * far_im + 1.0)
                factor = mask * (1.0 - amps[slot].astype(F32) / modulus)
                chi = rows_of(far_re * factor, far_im * factor)
                got_g[it, slot] = rows_of(*transform(four[1], four[0], chi))

    def backward(it, slot):
        @pl.when(not_last)
        def _():
            copy_g(it, slot).wait_recv()

        g = got_g[it, slot]
        for l in reversed(range(depth)):
            g_re, g_im = g[:PAT].astype(F32), g[PAT:].astype(F32)
            w_re, w_im = win[slot, l, 0], win[slot, l, 1]
            d = rows_of(w_re * g_re + w_im * g_im, w_re * g_im - w_im * g_re)
            if l > 0:
                g = rows_of(*transform(prop[1], prop[0], d))
                kept_g[slot, l - 1] = g
                continue

            @pl.when(not_first)
            def _():
                sent_g[it, slot] = rows_of(*transform(prop[1], prop[0], d))
                copy_g(it, slot).start()

    def accumulate(it, slot):
        for l in range(depth):
            g = got_g[it, slot] if l == depth - 1 else kept_g[slot, l]
            g_re, g_im = g[:PAT].astype(F32), g[PAT:].astype(F32)
            f_re = psi[it, slot, l, :PAT].astype(F32)
            f_im = psi[it, slot, l, PAT:].astype(F32)
            padded[0, pat : 2 * pat] = eights(f_re * g_re + f_im * g_im)
            padded[1, pat : 2 * pat] = eights(f_re * g_im - f_im * g_re)
            place = places[2, slot]
            for part in range(2):
                block = padded[part, pl.ds(place, reach + 1)]
                before = jnp.where(slot == 0, 0.0, grads[l, part])
                grads[l, part] = before + shifted(block, places[3, slot])

            @pl.when(slot == slots - 1)
            def _(l=l):
                @pl.when(has_after)
                def _():
                    sent_up[it, l] = flat(grads[l, :, own:]).astype(BF16)
                    copy_up(it, l).start()

                @pl.when(jnp.logical_and(has_before, it < ITERS - 1))
                def _():
                    sent_dn[it + 1, l] = flat(grads[l, :, :pat]).astype(BF16)
                    copy_dn(it + 1, l).start()

    lag = jnp.minimum(cuts - 1 - cut, 2)
    lag = jnp.where(lag == 2, slots - 1, lag)

    def step(index, _):
        it, at = index // (2 * slots - 1), index % (2 * slots - 1)

        @pl.when(at < slots)
        def _():
            forward(it, at)

        @pl.when(jnp.logical_and(at >= lag, at < lag + slots))
        def _():
            backward(it, at - lag)

        @pl.when(at >= slots - 1)
        def _():
            accumulate(it, at - (slots - 1))

        return 0

    lax.fori_loop(0, ITERS * (2 * slots - 1), step, 0)

    for l in reversed(range(depth)):
        @pl.when(has_before)
        def _(l=l):
            copy_up(ITERS - 1, l).wait_recv()

        out[l] = flat(updated(ITERS - 1, l))

    for it in range(ITERS):
        for slot in range(slots):
            @pl.when(not_last)
            def _(it=it, slot=slot):
                copy_psi(it, slot).wait_send()

            @pl.when(not_first)
            def _(it=it, slot=slot):
                copy_g(it, slot).wait_send()

        for l in range(depth):
            @pl.when(has_after)
            def _(it=it, l=l):
                copy_up(it, l).wait_send()

            @pl.when(jnp.logical_and(has_before, jnp.logical_or(not_first, it > 0)))
            def _(it=it, l=l):
                copy_dn(it, l).wait_send()


def local(object_slices, probe_field, row_offsets, columns, counts, amplitudes):
    depth, _, rows, width = object_slices.shape
    slots = amplitudes.shape[0]
    prop, four = tables(PAT)
    back = PAT - row_offsets
    places = jnp.stack([row_offsets // 8, row_offsets % 8, back // 8, back % 8])
    dma = pltpu.SemaphoreType.DMA
    vmem, smem = pltpu.VMEM, pltpu.SMEM
    return pl.pallas_call(
        kernel,
        out_shape=jax.ShapeDtypeStruct(object_slices.shape, F32),
        in_specs=[pl.BlockSpec(memory_space=smem)] * 2 + [pl.BlockSpec(memory_space=pl.ANY)] * 5,
        out_specs=pl.BlockSpec(memory_space=vmem),
        scratch_shapes=[
            vmem(object_slices.shape, F32),
            vmem(probe_field.shape, F32),
            vmem(amplitudes.shape, BF16),
            vmem(prop.shape, BF16),
            vmem(four.shape, BF16),
            vmem((depth, 2, (rows + PAT) // 8, 8, width), F32),
            vmem((depth, 2, (rows + PAT) // 8, 8, width), F32),
            vmem((2, (2 * PAT + rows) // 8 + 1, 8, width), F32),
            vmem((slots, depth, 2, PAT, width), F32),
            vmem((ITERS, slots, depth, 2 * PAT, PAT), BF16),
            vmem((slots, max(depth - 1, 1), 2 * PAT, PAT), BF16),
            vmem((ITERS, slots, 2 * PAT, PAT), BF16),
            vmem((ITERS, slots, 2 * PAT, PAT), BF16),
            vmem((ITERS, slots, 2 * PAT, PAT), BF16),
            vmem((ITERS, depth, 2, PAT, width), BF16),
            vmem((ITERS, depth, 2, PAT, width), BF16),
            vmem((ITERS, depth, 2, PAT, width), BF16),
            vmem((ITERS, depth, 2, PAT, width), BF16),
            dma((ITERS, slots)), dma((ITERS, slots)),
            dma((ITERS, slots)), dma((ITERS, slots)),
            dma((ITERS, depth)), dma((ITERS, depth)),
            dma((ITERS, depth)), dma((ITERS, depth)),
            dma((depth + 4,)), pltpu.SemaphoreType.REGULAR,
        ],
        compiler_params=pltpu.CompilerParams(
            collective_id=0, has_side_effects=True, vmem_limit_bytes=58 * 1024 * 1024),
    )(places, counts, object_slices, probe_field, amplitudes, jnp.asarray(prop), jnp.asarray(four))


def solution(mesh):
    in_specs = (
        P("cuts", None, "tile", None),
        P(),
        P("tile"),
        P("tile"),
        P("tile"),
        P("tile", None, None),
    )
    out_specs = P("cuts", None, "tile", None)
    return jax.shard_map(local, mesh=mesh, in_specs=in_specs, out_specs=out_specs, check_vma=False)
```

```python
import functools
import math

import jax
import jax.numpy as jnp
import numpy as np
from jax import lax
from jax.experimental import pallas as pl
from jax.experimental.pallas import tpu as pltpu
from jax.sharding import PartitionSpec as P

PAT = 256
HALF = PAT // 2
ITERS = 2
RATE = 0.25
BF16 = jnp.bfloat16
F32 = jnp.float32
MESH = pl.DeviceIdType.MESH


def tables(size):
    index = np.arange(size)
    angle = (index[:, None] * index[None, :] % size) * (2.0 * math.pi / size)
    cosine, sine = np.cos(angle), np.sin(angle)
    signed = np.where(index < size // 2, index, index - size)
    phase = (signed * signed % (8 * size)) * (-math.pi / (4.0 * size))
    filter_re, filter_im = np.cos(phase), np.sin(phase)
    kernel_re = (filter_re @ cosine - filter_im @ sine) / size
    kernel_im = (filter_re @ sine + filter_im @ cosine) / size
    offset = (index[:, None] - index[None, :]) % size
    norm = 1.0 / math.sqrt(size)

    def rounded(a):
        return a.astype(np.float32).astype(jnp.bfloat16)

    def four(re, im):
        re, im = rounded(re), rounded(im)
        left = np.concatenate([np.concatenate([re, -im], 1), np.concatenate([im, re], 1)], 0)
        right = np.concatenate([np.concatenate([re, im], 1), np.concatenate([-im, re], 1)], 0)
        rows = np.arange(2 * size).reshape(2, 2, size // 2).swapaxes(0, 1).reshape(-1)
        return np.stack([left[:, rows], right, right[:, rows], left])

    return four(kernel_re[offset], kernel_im[offset]), four(cosine * norm, -sine * norm)


def dot(left, right):
    return jnp.dot(left, right, preferred_element_type=F32)


def beside(mid):
    mid = mid.astype(BF16)
    return jnp.concatenate([mid[:PAT], mid[PAT:]], axis=1)


def halves(full):
    full = full.astype(BF16)
    return [stacked(full[h : h + HALF, :PAT], full[h : h + HALF, PAT:]) for h in (0, HALF)]


def stacked(re, im):
    return jnp.concatenate([re.astype(BF16), im.astype(BF16)], axis=0)


def transform(tabs, which, field):
    mid = dot(tabs[which], jnp.concatenate(field, axis=0))
    return dot(beside(mid), tabs[which + 1])


def shifted(block, shift):
    turned = pltpu.roll(block, (8 - shift) & 7, 1)
    within = lax.broadcasted_iota(jnp.int32, turned[1:].shape, 1) < 8 - shift
    return jnp.where(within, turned[:-1], turned[1:])


def kernel(
    places, counts, obj_in, probe_in, amps_in, prop_in, four_in, out,
    obj, probe, amps, prop, four, ext, grads, padded, win, psi, kept_g, sent_psi, got_g, sent_g, sent_dn, sent_up, got_dn, got_up,
    psi_ss, psi_rs, g_ss, g_rs, dn_ss, dn_rs, up_ss, up_rs,
    in_sems, go,
):
    depth, _, rows, width = obj.shape
    slots = amps.shape[0]
    own, reach, pat = rows // 8, (rows + PAT) // 8, PAT // 8
    cut, cuts = lax.axis_index("cuts"), lax.axis_size("cuts")
    tile, tiles = lax.axis_index("tile"), lax.axis_size("tile")
    not_first, not_last = cut > 0, cut < cuts - 1
    has_before, has_after = tile > 0, tile < tiles - 1

    slice_loads = [
        pltpu.make_async_copy(obj_in.at[l], obj.at[l], in_sems.at[l]) for l in range(depth)
    ]
    loads = [
        pltpu.make_async_copy(src, dst, in_sems.at[depth + i])
        for i, (src, dst) in enumerate(
            ((prop_in, prop), (probe_in, probe), (four_in, four), (amps_in, amps)))
    ]
    for load in slice_loads + loads:
        load.start()

    barrier = pltpu.get_barrier_semaphore()
    for there, where in (
        (not_first, {"cuts": cut - 1}),
        (not_last, {"cuts": cut + 1}),
        (has_before, {"tile": tile - 1}),
        (has_after, {"tile": tile + 1}),
    ):
        @pl.when(there)
        def _(where=where):
            pl.semaphore_signal(barrier, inc=1, device_id=where, device_id_type=MESH)
    neighbours = sum(
        there.astype(jnp.int32) for there in (not_first, not_last, has_before, has_after)
    )
    pl.semaphore_wait(barrier, neighbours)

    def copy_psi(it, slot, h):
        return pltpu.make_async_remote_copy(
            sent_psi.at[it, slot, h], psi.at[it, slot, 0, h],
            psi_ss.at[it, slot, h], psi_rs.at[it, slot, h],
            device_id={"cuts": cut + 1}, device_id_type=MESH)

    def copy_g(it, slot, h):
        return pltpu.make_async_remote_copy(
            sent_g.at[it, slot, h], got_g.at[it, slot, h],
            g_ss.at[it, slot, h], g_rs.at[it, slot, h],
            device_id={"cuts": cut - 1}, device_id_type=MESH)

    def copy_dn(stage, l):
        return pltpu.make_async_remote_copy(
            sent_dn.at[stage, l], got_dn.at[stage, l], dn_ss.at[stage, l], dn_rs.at[stage, l],
            device_id={"tile": tile - 1}, device_id_type=MESH)

    def copy_up(it, l):
        return pltpu.make_async_remote_copy(
            sent_up.at[it, l], got_up.at[it, l], up_ss.at[it, l], up_rs.at[it, l],
            device_id={"tile": tile + 1}, device_id_type=MESH)

    for l in range(depth):
        slice_loads[l].wait()
        sent_dn[0, l] = obj[l, :, :PAT].astype(BF16)
        if l == 0:
            @pl.when(cut == 1)
            def _():
                pl.semaphore_wait(go, 1)

        @pl.when(has_before)
        def _(l=l):
            copy_dn(0, l).start()

    for load in loads:
        load.wait()

    for stage in range(ITERS):
        @pl.when(jnp.logical_not(has_after))
        def _(stage=stage):
            got_dn[stage] = jnp.zeros(got_dn.shape[1:], BF16)

        @pl.when(jnp.logical_not(has_before))
        def _(stage=stage):
            got_up[stage] = jnp.zeros(got_up.shape[1:], BF16)

    @pl.when(jnp.logical_not(not_first))
    def _():
        for h in range(2):
            at = pl.ds(h * HALF, HALF)
            start = stacked(probe[0, at], probe[1, at])
            for it in range(ITERS):
                for slot in range(slots):
                    psi[it, slot, 0, h] = start

        @pl.when(has_before)
        def _():
            for l in range(depth):
                copy_dn(0, l).wait_send()

        if cuts > 1:
            pl.semaphore_signal(go, inc=1, device_id={"cuts": cut + 1}, device_id_type=MESH)

    for part in range(2):
        padded[part, :pat] = jnp.zeros((pat, 8, width), F32)
        padded[part, 2 * pat :] = jnp.zeros((own + 1, 8, width), F32)

    def eights(block):
        return block.reshape(block.shape[:-2] + (block.shape[-2] // 8, 8, width))

    def flat(block):
        return block.reshape(block.shape[:-3] + (block.shape[-3] * 8, width))

    def prepare(it, l):
        @pl.when(has_after)
        def _():
            copy_dn(it, l).wait_recv()

        @pl.when(it == 0)
        def _():
            ext[l, :, :own] = eights(obj[l])
            ext[l, :, own:] = eights(got_dn[0, l].astype(F32))

        @pl.when(it > 0)
        def _():
            @pl.when(has_before)
            def _():
                copy_up(it - 1, l).wait_recv()

            ext[l, :, :own] = updated(it - 1, l)
            ext[l, :, own:] -= RATE * (grads[l, :, own:] + eights(got_dn[it, l].astype(F32)))

    def extract(slot, l):
        place = places[0, slot]
        for part in range(2):
            block = ext[l, part, pl.ds(place, pat + 1)]
            win[slot, l, part] = flat(shifted(block, places[1, slot]))

    def updated(it, l):
        top = ext[l, :, :pat] - RATE * (grads[l, :, :pat] + eights(got_up[it, l].astype(F32)))
        if own == pat:
            return top
        rest = ext[l, :, pat:own] - RATE * grads[l, :, pat:own]
        return jnp.concatenate([top, rest], axis=1)

    def forward(it, slot):
        @pl.when(jnp.logical_and(not_first, slot == 0))
        def _():
            for l in range(depth):
                prepare(it, l)
                for each in range(slots):
                    extract(each, l)

        for l in range(depth):
            @pl.when(jnp.logical_not(not_first))
            def _(l=l):
                @pl.when(slot == 0)
                def _():
                    prepare(it, l)

                extract(slot, l)

            field, mid = [], 0.0
            for h in range(2):
                if l == 0:
                    @pl.when(not_first)
                    def _(h=h):
                        copy_psi(it, slot, h).wait_recv()

                at = pl.ds(h * HALF, HALF)
                w_re, w_im = win[slot, l, 0, at], win[slot, l, 1, at]
                f_re = psi[it, slot, l, h, :HALF].astype(F32)
                f_im = psi[it, slot, l, h, HALF:].astype(F32)
                field.append(stacked(f_re * w_re - f_im * w_im, f_re * w_im + f_im * w_re))
                if l < depth - 1:
                    mid += dot(prop[0, :, h * PAT : (h + 1) * PAT], field[h])

            if l < depth - 1:
                for h, half in enumerate(halves(dot(beside(mid), prop[1]))):
                    psi[it, slot, l + 1, h] = half
                continue

            @pl.when(not_last)
            def _():
                mid = beside(dot(prop[0], jnp.concatenate(field, axis=0)))
                for h in range(2):
                    full = dot(mid[h * HALF : (h + 1) * HALF], prop[1])
                    sent_psi[it, slot, h] = stacked(full[:, :PAT], full[:, PAT:])
                    copy_psi(it, slot, h).start()

            @pl.when(jnp.logical_not(not_last))
            def _():
                far = transform(four, 0, field)
                far_re, far_im = far[:, :PAT], far[:, PAT:]
                mask = jnp.where(slot < counts[0], 1.0, 0.0).astype(F32)
                modulus = jnp.sqrt(far_re * far_re + far_im * far_im + 1.0)
                factor = mask * (1.0 - amps[slot].astype(F32) / modulus)
                chi = halves(jnp.concatenate([far_re * factor, far_im * factor], axis=1))
                for h, half in enumerate(halves(transform(four, 2, chi))):
                    kept_g[slot, l, h] = half

    def backward(it, slot):
        @pl.when(not_last)
        def _():
            mid = 0.0
            for h in range(2):
                copy_g(it, slot, h).wait_recv()
                mid += dot(prop[2, :, h * PAT : (h + 1) * PAT], got_g[it, slot, h])
            for h, half in enumerate(halves(dot(beside(mid), prop[3]))):
                kept_g[slot, depth - 1, h] = half

        def adjoint(l, h):
            at = pl.ds(h * HALF, HALF)
            w_re, w_im = win[slot, l, 0, at], win[slot, l, 1, at]
            g_re = kept_g[slot, l, h, :HALF].astype(F32)
            g_im = kept_g[slot, l, h, HALF:].astype(F32)
            return stacked(w_re * g_re + w_im * g_im, w_re * g_im - w_im * g_re)

        for l in reversed(range(1, depth)):
            full = transform(prop, 2, [adjoint(l, 0), adjoint(l, 1)])
            for h, half in enumerate(halves(full)):
                kept_g[slot, l - 1, h] = half

        @pl.when(not_first)
        def _():
            for h in range(2):
                sent_g[it, slot, h] = adjoint(0, h)
                copy_g(it, slot, h).start()

    def accumulate(it, slot):
        for l in range(depth):
            for h in range(2):
                g_re = kept_g[slot, l, h, :HALF].astype(F32)
                g_im = kept_g[slot, l, h, HALF:].astype(F32)
                f_re = psi[it, slot, l, h, :HALF].astype(F32)
                f_im = psi[it, slot, l, h, HALF:].astype(F32)
                at = pl.ds(pat + h * (pat // 2), pat // 2)
                padded[0, at] = eights(f_re * g_re + f_im * g_im)
                padded[1, at] = eights(f_re * g_im - f_im * g_re)
            place = places[2, slot]
            for part in range(2):
                block = padded[part, pl.ds(place, reach + 1)]
                before = jnp.where(slot == 0, 0.0, grads[l, part])
                grads[l, part] = before + shifted(block, places[3, slot])

            @pl.when(slot == slots - 1)
            def _(l=l):
                @pl.when(has_after)
                def _():
                    sent_up[it, l] = flat(grads[l, :, own:]).astype(BF16)
                    copy_up(it, l).start()

                @pl.when(jnp.logical_and(has_before, it < ITERS - 1))
                def _():
                    sent_dn[it + 1, l] = flat(grads[l, :, :pat]).astype(BF16)
                    copy_dn(it + 1, l).start()

    lag = jnp.minimum(cuts - 1 - cut, 2)
    lag = jnp.where(lag == 2, slots - 1, lag)

    def step(index, _):
        it, at = index // (2 * slots - 1), index % (2 * slots - 1)

        @pl.when(at < slots)
        def _():
            forward(it, at)

        @pl.when(jnp.logical_and(at >= lag, at < lag + slots))
        def _():
            backward(it, at - lag)

        @pl.when(at >= slots - 1)
        def _():
            accumulate(it, at - (slots - 1))

        return 0

    lax.fori_loop(0, ITERS * (2 * slots - 1), step, 0)

    for l in reversed(range(depth)):
        @pl.when(has_before)
        def _(l=l):
            copy_up(ITERS - 1, l).wait_recv()

        out[l] = flat(updated(ITERS - 1, l))

    for it in range(ITERS):
        for slot in range(slots):
            @pl.when(not_last)
            def _(it=it, slot=slot):
                for h in range(2):
                    copy_psi(it, slot, h).wait_send()

            @pl.when(not_first)
            def _(it=it, slot=slot):
                for h in range(2):
                    copy_g(it, slot, h).wait_send()

        for l in range(depth):
            @pl.when(has_after)
            def _(it=it, l=l):
                copy_up(it, l).wait_send()

            @pl.when(jnp.logical_and(has_before, jnp.logical_or(not_first, it > 0)))
            def _(it=it, l=l):
                copy_dn(it, l).wait_send()


def local(object_slices, probe_field, row_offsets, columns, counts, amplitudes):
    depth, _, rows, width = object_slices.shape
    slots = amplitudes.shape[0]
    prop, four = tables(PAT)
    back = PAT - row_offsets
    places = jnp.stack([row_offsets // 8, row_offsets % 8, back // 8, back % 8])
    dma = pltpu.SemaphoreType.DMA
    vmem, smem = pltpu.VMEM, pltpu.SMEM
    return pl.pallas_call(
        kernel,
        out_shape=jax.ShapeDtypeStruct(object_slices.shape, F32),
        in_specs=[pl.BlockSpec(memory_space=smem)] * 2 + [pl.BlockSpec(memory_space=pl.ANY)] * 5,
        out_specs=pl.BlockSpec(memory_space=vmem),
        scratch_shapes=[
            vmem(object_slices.shape, F32),
            vmem(probe_field.shape, F32),
            vmem(amplitudes.shape, BF16),
            vmem(prop.shape, BF16),
            vmem(four.shape, BF16),
            vmem((depth, 2, (rows + PAT) // 8, 8, width), F32),
            vmem((depth, 2, (rows + PAT) // 8, 8, width), F32),
            vmem((2, (2 * PAT + rows) // 8 + 1, 8, width), F32),
            vmem((slots, depth, 2, PAT, width), F32),
            vmem((ITERS, slots, depth, 2, PAT, PAT), BF16),
            vmem((slots, depth, 2, PAT, PAT), BF16),
            vmem((ITERS, slots, 2, PAT, PAT), BF16),
            vmem((ITERS, slots, 2, PAT, PAT), BF16),
            vmem((ITERS, slots, 2, PAT, PAT), BF16),
            vmem((ITERS, depth, 2, PAT, width), BF16),
            vmem((ITERS, depth, 2, PAT, width), BF16),
            vmem((ITERS, depth, 2, PAT, width), BF16),
            vmem((ITERS, depth, 2, PAT, width), BF16),
            dma((ITERS, slots, 2)), dma((ITERS, slots, 2)),
            dma((ITERS, slots, 2)), dma((ITERS, slots, 2)),
            dma((ITERS, depth)), dma((ITERS, depth)),
            dma((ITERS, depth)), dma((ITERS, depth)),
            dma((depth + 4,)), pltpu.SemaphoreType.REGULAR,
        ],
        compiler_params=pltpu.CompilerParams(
            collective_id=0, has_side_effects=True, vmem_limit_bytes=58 * 1024 * 1024),
    )(places, counts, object_slices, probe_field, amplitudes, jnp.asarray(prop), jnp.asarray(four))


def solution(mesh):
    in_specs = (
        P("cuts", None, "tile", None),
        P(),
        P("tile"),
        P("tile"),
        P("tile"),
        P("tile", None, None),
    )
    out_specs = P("cuts", None, "tile", None)
    return jax.shard_map(local, mesh=mesh, in_specs=in_specs, out_specs=out_specs, check_vma=False)
```

```python
import functools
import math

import jax
import jax.numpy as jnp
import numpy as np
from jax import lax
from jax.experimental import pallas as pl
from jax.experimental.pallas import tpu as pltpu
from jax.sharding import PartitionSpec as P

PAT = 256
HALF = PAT // 2
ITERS = 2
RATE = 0.25
BF16 = jnp.bfloat16
F32 = jnp.float32
MESH = pl.DeviceIdType.MESH


def tables(size):
    index = np.arange(size)
    angle = (index[:, None] * index[None, :] % size) * (2.0 * math.pi / size)
    cosine, sine = np.cos(angle), np.sin(angle)
    signed = np.where(index < size // 2, index, index - size)
    phase = (signed * signed % (8 * size)) * (-math.pi / (4.0 * size))
    filter_re, filter_im = np.cos(phase), np.sin(phase)
    kernel_re = (filter_re @ cosine - filter_im @ sine) / size
    kernel_im = (filter_re @ sine + filter_im @ cosine) / size
    offset = (index[:, None] - index[None, :]) % size
    norm = 1.0 / math.sqrt(size)

    def rounded(a):
        return a.astype(np.float32).astype(jnp.bfloat16)

    def four(re, im):
        re, im = rounded(re), rounded(im)
        left = np.concatenate([np.concatenate([re, -im], 1), np.concatenate([im, re], 1)], 0)
        right = np.concatenate([np.concatenate([re, im], 1), np.concatenate([-im, re], 1)], 0)
        rows = np.arange(2 * size).reshape(2, 2, size // 2).swapaxes(0, 1).reshape(-1)
        return np.stack([left[:, rows], right, right[:, rows], left])

    return four(kernel_re[offset], kernel_im[offset]), four(cosine * norm, -sine * norm)


def dot(left, right):
    return jnp.dot(left, right, preferred_element_type=F32)


def beside(mid):
    mid = mid.astype(BF16)
    return jnp.concatenate([mid[:PAT], mid[PAT:]], axis=1)


def halves(full):
    full = full.astype(BF16)
    return [stacked(full[h : h + HALF, :PAT], full[h : h + HALF, PAT:]) for h in (0, HALF)]


def stacked(re, im):
    return jnp.concatenate([re.astype(BF16), im.astype(BF16)], axis=0)


def transform(tabs, which, field):
    field = jnp.concatenate(field, axis=0)
    mid_re = dot(tabs[which, :PAT], field).astype(BF16)
    mid_im = dot(tabs[which, PAT:], field).astype(BF16)
    return dot(mid_re, tabs[which + 1, :PAT]) + dot(mid_im, tabs[which + 1, PAT:])


def shifted(block, shift):
    turned = pltpu.roll(block, (8 - shift) & 7, 1)
    within = lax.broadcasted_iota(jnp.int32, turned[1:].shape, 1) < 8 - shift
    return jnp.where(within, turned[:-1], turned[1:])


def kernel(
    places, counts, obj_in, probe_in, amps_in, prop_in, four_in, out,
    obj, probe, amps, prop, four, ext, grads, padded, win, psi, kept_g, sent_psi, got_g, sent_g, sent_dn, sent_up, got_dn, got_up,
    psi_ss, psi_rs, g_ss, g_rs, dn_ss, dn_rs, up_ss, up_rs,
    in_sems, go,
):
    depth, _, rows, width = obj.shape
    slots = amps.shape[0]
    own, reach, pat = rows // 8, (rows + PAT) // 8, PAT // 8
    cut, cuts = lax.axis_index("cuts"), lax.axis_size("cuts")
    tile, tiles = lax.axis_index("tile"), lax.axis_size("tile")
    not_first, not_last = cut > 0, cut < cuts - 1
    has_before, has_after = tile > 0, tile < tiles - 1

    slice_loads = [
        pltpu.make_async_copy(obj_in.at[l], obj.at[l], in_sems.at[l]) for l in range(depth)
    ]
    loads = [
        pltpu.make_async_copy(src, dst, in_sems.at[depth + i])
        for i, (src, dst) in enumerate(
            ((prop_in, prop), (probe_in, probe), (four_in, four), (amps_in, amps)))
    ]
    for load in slice_loads + loads:
        load.start()

    barrier = pltpu.get_barrier_semaphore()
    for there, where in (
        (not_first, {"cuts": cut - 1}),
        (not_last, {"cuts": cut + 1}),
        (has_before, {"tile": tile - 1}),
        (has_after, {"tile": tile + 1}),
    ):
        @pl.when(there)
        def _(where=where):
            pl.semaphore_signal(barrier, inc=1, device_id=where, device_id_type=MESH)
    neighbours = sum(
        there.astype(jnp.int32) for there in (not_first, not_last, has_before, has_after)
    )
    pl.semaphore_wait(barrier, neighbours)

    def copy_psi(it, slot, h):
        return pltpu.make_async_remote_copy(
            sent_psi.at[it, slot, h], psi.at[it, slot, 0, h],
            psi_ss.at[it, slot, h], psi_rs.at[it, slot, h],
            device_id={"cuts": cut + 1}, device_id_type=MESH)

    def copy_g(it, slot, h):
        return pltpu.make_async_remote_copy(
            sent_g.at[it, slot, h], got_g.at[it, slot, h],
            g_ss.at[it, slot, h], g_rs.at[it, slot, h],
            device_id={"cuts": cut - 1}, device_id_type=MESH)

    def copy_dn(stage, l):
        return pltpu.make_async_remote_copy(
            sent_dn.at[stage, l], got_dn.at[stage, l], dn_ss.at[stage, l], dn_rs.at[stage, l],
            device_id={"tile": tile - 1}, device_id_type=MESH)

    def copy_up(it, l):
        return pltpu.make_async_remote_copy(
            sent_up.at[it, l], got_up.at[it, l], up_ss.at[it, l], up_rs.at[it, l],
            device_id={"tile": tile + 1}, device_id_type=MESH)

    for l in range(depth):
        slice_loads[l].wait()
        sent_dn[0, l] = obj[l, :, :PAT].astype(BF16)
        if l == 0:
            @pl.when(cut == 1)
            def _():
                pl.semaphore_wait(go, 1)

        @pl.when(has_before)
        def _(l=l):
            copy_dn(0, l).start()

    for load in loads:
        load.wait()

    for stage in range(ITERS):
        @pl.when(jnp.logical_not(has_after))
        def _(stage=stage):
            got_dn[stage] = jnp.zeros(got_dn.shape[1:], BF16)

        @pl.when(jnp.logical_not(has_before))
        def _(stage=stage):
            got_up[stage] = jnp.zeros(got_up.shape[1:], BF16)

    @pl.when(jnp.logical_not(not_first))
    def _():
        for h in range(2):
            at = pl.ds(h * HALF, HALF)
            start = stacked(probe[0, at], probe[1, at])
            for it in range(ITERS):
                for slot in range(slots):
                    psi[it, slot, 0, h] = start

        @pl.when(has_before)
        def _():
            for l in range(depth):
                copy_dn(0, l).wait_send()

        if cuts > 1:
            pl.semaphore_signal(go, inc=1, device_id={"cuts": cut + 1}, device_id_type=MESH)

    for part in range(2):
        padded[part, :pat] = jnp.zeros((pat, 8, width), F32)
        padded[part, 2 * pat :] = jnp.zeros((own + 1, 8, width), F32)

    def eights(block):
        return block.reshape(block.shape[:-2] + (block.shape[-2] // 8, 8, width))

    def flat(block):
        return block.reshape(block.shape[:-3] + (block.shape[-3] * 8, width))

    def prepare(it, l):
        @pl.when(has_after)
        def _():
            copy_dn(it, l).wait_recv()

        @pl.when(it == 0)
        def _():
            ext[l, :, :own] = eights(obj[l])
            ext[l, :, own:] = eights(got_dn[0, l].astype(F32))

        @pl.when(it > 0)
        def _():
            @pl.when(has_before)
            def _():
                copy_up(it - 1, l).wait_recv()

            ext[l, :, :own] = updated(it - 1, l)
            ext[l, :, own:] -= RATE * (grads[l, :, own:] + eights(got_dn[it, l].astype(F32)))

    def extract(slot, l):
        place = places[0, slot]
        for part in range(2):
            block = ext[l, part, pl.ds(place, pat + 1)]
            win[slot, l, part] = flat(shifted(block, places[1, slot]))

    def updated(it, l):
        top = ext[l, :, :pat] - RATE * (grads[l, :, :pat] + eights(got_up[it, l].astype(F32)))
        if own == pat:
            return top
        rest = ext[l, :, pat:own] - RATE * grads[l, :, pat:own]
        return jnp.concatenate([top, rest], axis=1)

    def forward(it, slot):
        @pl.when(jnp.logical_and(not_first, slot == 0))
        def _():
            for l in range(depth):
                prepare(it, l)
                for each in range(slots):
                    extract(each, l)

        for l in range(depth):
            @pl.when(jnp.logical_not(not_first))
            def _(l=l):
                @pl.when(slot == 0)
                def _():
                    prepare(it, l)

                extract(slot, l)

            field, mid = [], None
            for h in range(2):
                if l == 0:
                    @pl.when(not_first)
                    def _(h=h):
                        copy_psi(it, slot, h).wait_recv()

                at = pl.ds(h * HALF, HALF)
                w_re, w_im = win[slot, l, 0, at], win[slot, l, 1, at]
                f_re = psi[it, slot, l, h, :HALF].astype(F32)
                f_im = psi[it, slot, l, h, HALF:].astype(F32)
                field.append(stacked(f_re * w_re - f_im * w_im, f_re * w_im + f_im * w_re))
                if l < depth - 1:
                    term = dot(prop[0, :, h * PAT : (h + 1) * PAT], field[h])
                    mid = term if mid is None else mid + term

            if l < depth - 1:
                for h, half in enumerate(halves(dot(beside(mid), prop[1]))):
                    psi[it, slot, l + 1, h] = half
                continue

            @pl.when(not_last)
            def _():
                mid = beside(dot(prop[0], jnp.concatenate(field, axis=0)))
                for h in range(2):
                    full = dot(mid[h * HALF : (h + 1) * HALF], prop[1])
                    sent_psi[it, slot, h] = stacked(full[:, :PAT], full[:, PAT:])
                    copy_psi(it, slot, h).start()

            @pl.when(jnp.logical_not(not_last))
            def _():
                far = transform(four, 0, field)
                far_re, far_im = far[:, :PAT], far[:, PAT:]
                mask = jnp.where(slot < counts[0], 1.0, 0.0).astype(F32)
                modulus = jnp.sqrt(far_re * far_re + far_im * far_im + 1.0)
                factor = mask * (1.0 - amps[slot].astype(F32) / modulus)
                chi = halves(jnp.concatenate([far_re * factor, far_im * factor], axis=1))
                for h, half in enumerate(halves(transform(four, 2, chi))):
                    kept_g[slot, l, h] = half

    def backward(it, slot):
        @pl.when(not_last)
        def _():
            mid = None
            for h in range(2):
                copy_g(it, slot, h).wait_recv()
                term = dot(prop[2, :, h * PAT : (h + 1) * PAT], got_g[it, slot, h])
                mid = term if mid is None else mid + term
            for h, half in enumerate(halves(dot(beside(mid), prop[3]))):
                kept_g[slot, depth - 1, h] = half

        def adjoint(l, h):
            at = pl.ds(h * HALF, HALF)
            w_re, w_im = win[slot, l, 0, at], win[slot, l, 1, at]
            g_re = kept_g[slot, l, h, :HALF].astype(F32)
            g_im = kept_g[slot, l, h, HALF:].astype(F32)
            return stacked(w_re * g_re + w_im * g_im, w_re * g_im - w_im * g_re)

        for l in reversed(range(1, depth)):
            full = transform(prop, 2, [adjoint(l, 0), adjoint(l, 1)])
            for h, half in enumerate(halves(full)):
                kept_g[slot, l - 1, h] = half

        @pl.when(not_first)
        def _():
            for h in range(2):
                sent_g[it, slot, h] = adjoint(0, h)
                copy_g(it, slot, h).start()

    def accumulate(it, slot):
        for l in range(depth):
            for h in range(2):
                g_re = kept_g[slot, l, h, :HALF].astype(F32)
                g_im = kept_g[slot, l, h, HALF:].astype(F32)
                f_re = psi[it, slot, l, h, :HALF].astype(F32)
                f_im = psi[it, slot, l, h, HALF:].astype(F32)
                at = pl.ds(pat + h * (pat // 2), pat // 2)
                padded[0, at] = eights(f_re * g_re + f_im * g_im)
                padded[1, at] = eights(f_re * g_im - f_im * g_re)
            place = places[2, slot]
            for part in range(2):
                block = padded[part, pl.ds(place, reach + 1)]
                before = jnp.where(slot == 0, 0.0, grads[l, part])
                grads[l, part] = before + shifted(block, places[3, slot])

            @pl.when(slot == slots - 1)
            def _(l=l):
                @pl.when(has_after)
                def _():
                    sent_up[it, l] = flat(grads[l, :, own:]).astype(BF16)
                    copy_up(it, l).start()

                @pl.when(jnp.logical_and(has_before, it < ITERS - 1))
                def _():
                    sent_dn[it + 1, l] = flat(grads[l, :, :pat]).astype(BF16)
                    copy_dn(it + 1, l).start()

    lag = jnp.minimum(cuts - 1 - cut, 2)
    lag = jnp.where(lag == 2, slots - 1, lag)

    def step(index, _):
        it, at = index // (2 * slots - 1), index % (2 * slots - 1)

        @pl.when(at < slots)
        def _():
            forward(it, at)

        @pl.when(jnp.logical_and(at >= lag, at < lag + slots))
        def _():
            backward(it, at - lag)

        @pl.when(at >= slots - 1)
        def _():
            accumulate(it, at - (slots - 1))

        return 0

    lax.fori_loop(0, ITERS * (2 * slots - 1), step, 0)

    for l in reversed(range(depth)):
        @pl.when(has_before)
        def _(l=l):
            copy_up(ITERS - 1, l).wait_recv()

        out[l] = flat(updated(ITERS - 1, l))

    for it in range(ITERS):
        for slot in range(slots):
            @pl.when(not_last)
            def _(it=it, slot=slot):
                for h in range(2):
                    copy_psi(it, slot, h).wait_send()

            @pl.when(not_first)
            def _(it=it, slot=slot):
                for h in range(2):
                    copy_g(it, slot, h).wait_send()

        for l in range(depth):
            @pl.when(has_after)
            def _(it=it, l=l):
                copy_up(it, l).wait_send()

            @pl.when(jnp.logical_and(has_before, jnp.logical_or(not_first, it > 0)))
            def _(it=it, l=l):
                copy_dn(it, l).wait_send()


def local(object_slices, probe_field, row_offsets, columns, counts, amplitudes):
    depth, _, rows, width = object_slices.shape
    slots = amplitudes.shape[0]
    prop, four = tables(PAT)
    back = PAT - row_offsets
    places = jnp.stack([row_offsets // 8, row_offsets % 8, back // 8, back % 8])
    dma = pltpu.SemaphoreType.DMA
    vmem, smem = pltpu.VMEM, pltpu.SMEM
    return pl.pallas_call(
        kernel,
        out_shape=jax.ShapeDtypeStruct(object_slices.shape, F32),
        in_specs=[pl.BlockSpec(memory_space=smem)] * 2 + [pl.BlockSpec(memory_space=pl.ANY)] * 5,
        out_specs=pl.BlockSpec(memory_space=vmem),
        scratch_shapes=[
            vmem(object_slices.shape, F32),
            vmem(probe_field.shape, F32),
            vmem(amplitudes.shape, BF16),
            vmem(prop.shape, BF16),
            vmem(four.shape, BF16),
            vmem((depth, 2, (rows + PAT) // 8, 8, width), F32),
            vmem((depth, 2, (rows + PAT) // 8, 8, width), F32),
            vmem((2, (2 * PAT + rows) // 8 + 1, 8, width), F32),
            vmem((slots, depth, 2, PAT, width), F32),
            vmem((ITERS, slots, depth, 2, PAT, PAT), BF16),
            vmem((slots, depth, 2, PAT, PAT), BF16),
            vmem((ITERS, slots, 2, PAT, PAT), BF16),
            vmem((ITERS, slots, 2, PAT, PAT), BF16),
            vmem((ITERS, slots, 2, PAT, PAT), BF16),
            vmem((ITERS, depth, 2, PAT, width), BF16),
            vmem((ITERS, depth, 2, PAT, width), BF16),
            vmem((ITERS, depth, 2, PAT, width), BF16),
            vmem((ITERS, depth, 2, PAT, width), BF16),
            dma((ITERS, slots, 2)), dma((ITERS, slots, 2)),
            dma((ITERS, slots, 2)), dma((ITERS, slots, 2)),
            dma((ITERS, depth)), dma((ITERS, depth)),
            dma((ITERS, depth)), dma((ITERS, depth)),
            dma((depth + 4,)), pltpu.SemaphoreType.REGULAR,
        ],
        compiler_params=pltpu.CompilerParams(
            collective_id=0, has_side_effects=True, vmem_limit_bytes=58 * 1024 * 1024),
    )(places, counts, object_slices, probe_field, amplitudes, jnp.asarray(prop), jnp.asarray(four))


def solution(mesh):
    in_specs = (
        P("cuts", None, "tile", None),
        P(),
        P("tile"),
        P("tile"),
        P("tile"),
        P("tile", None, None),
    )
    out_specs = P("cuts", None, "tile", None)
    return jax.shard_map(local, mesh=mesh, in_specs=in_specs, out_specs=out_specs, check_vma=False)
```
